256 devices in a mesh: prow: 16 (over z, core), pcol: 16 (over y, x).
Axes of the slice: x: 4, y: 4, z: 8, core: 2. Of those that a mesh axis runs over, the one named last changes fastest.
Arguments:
- inverse_block: float32 [20480, 20480], P('prow', 'pcol'), may hold values from -6 to 6
- l_panel: float32 [20480, 512], P(('prow', 'pcol')), may hold values from -0.0625 to 0.0625
- d_inverse: float32 [2, 256, 256], replicated, may hold values from -6 to 6
- owner_map: int32 [80], replicated, may hold values from 0 to 79, each once
- ancestors: int32 [2, 40], replicated, may hold values from 0 to 79, as said below
Outputs:
- inverse_column: float32 [20480, 512], P(('prow', 'pcol'))
- diag_inverse: float32 [2, 256, 256], replicated
The draws below stay inside these ranges and needn't reach their ends.
Inputs may be any that keep to these rules, and one draw needn't show every extreme that they name: `ancestors`: each row holds 40 different block numbers in rising order; the two rows together hold every block number exactly once. `owner_map`: each block number appears once.
All inputs are finite; a program needn't handle non-finite values.
Results may differ from the reference program's by a relative error of at most 0.000075.
Values sent between devices are 32-bit elements; how exact they have to be, the bound alone decides.
No kernel may reach another device: no remote copies, remote signals or barrier semaphores. Data moves between devices by JAX's collectives and lax.ppermute only.
A program may use at most 64 MiB of HBM per device.

```python
import jax
import jax.numpy as jnp
from jax import lax

B = 256
NA = 20480
NBLK = 80
NANC = 40


def draw_ancestors(key, part):
    key = jax.random.fold_in(key, 7)
    order = jax.random.permutation(key, NBLK).astype(jnp.int32)
    first = jnp.sort(order[:NANC])
    second = jnp.sort(order[NANC:2 * NANC])
    return jnp.stack([first, second]).astype(jnp.int32)


def level_of(stream_key, dims, cuts, least, high):
    def one(position, shards_of):
        draws = jax.random.uniform(jax.random.fold_in(jax.random.fold_in(stream_key, 6), position), (shards_of,), jnp.float32, least / len(cuts), high / len(cuts))
        return jnp.repeat(jnp.exp(draws), dims[position] // shards_of).reshape((-1,) + (1,) * (len(dims) - position - 1))

    loudness = one(*cuts[0])
    for cut in cuts[1:]:
        loudness = loudness * one(*cut)
    return loudness


def gaussian(rng, extent, scale, reach, cuts=(), dtype=jnp.bfloat16):
    gain = level_of(rng, extent, cuts, -0.22, 0.18) if cuts else 1.0
    drawn = jax.random.normal(rng, extent, jnp.float32) * scale * gain
    return jnp.minimum(jnp.maximum(drawn, -reach), reach).astype(dtype)


def setup_inputs(seed: int = 0) -> dict:
    splits = jax.random.split(jax.random.key(seed), 6)
    return {
        "inverse_block": gaussian(splits[0], (NA, NA), 1.0, 6.0, ((0, 16), (1, 16)), jnp.float32),
        "l_panel": gaussian(splits[1], (NA, 2 * B), (NA // 2) ** -0.5, 0.0625, ((0, 256),), jnp.float32),
        "d_inverse": gaussian(splits[2], (2, B, B), 1.0, 6.0, (), jnp.float32),
        "owner_map": jax.random.permutation(splits[3], NBLK).astype(jnp.int32),
        "ancestors": draw_ancestors(jax.random.fold_in(splits[5], 71), 0),
    }


def reference(inverse_block, l_panel, d_inverse, owner_map, ancestors):
    in_set = jnp.any(owner_map[None, :, None] == ancestors[:, None, :], axis=2).astype(jnp.float32)
    row_mask = jnp.repeat(in_set.T, B, axis=0)
    masked = (l_panel.reshape(NA, 2, B) * row_mask[:, :, None]).reshape(NA, 2 * B)
    product = -jnp.dot(inverse_block, masked, precision=lax.Precision.HIGHEST, preferred_element_type=jnp.float32)
    column = (product.reshape(NA, 2, B) * row_mask[:, :, None]).reshape(NA, 2 * B)
    terms = jnp.einsum("rkb,rkc->kbc", masked.reshape(NA, 2, B), column.reshape(NA, 2, B), precision=lax.Precision.HIGHEST)
    return column, d_inverse - terms
```

```python
import functools

import jax
import jax.numpy as jnp
from jax import lax
from jax.experimental import pallas as pl
from jax.experimental.pallas import tpu as pltpu
from jax.sharding import PartitionSpec as P

ROW, COL = "prow", "pcol"


def split(x):
    high = x.astype(jnp.bfloat16)
    low = (x - high.astype(jnp.float32)).astype(jnp.bfloat16)
    return high, low


def dot(a, b, contract):
    return lax.dot_general(a, b, ((contract, (0,)), ((), ())), preferred_element_type=jnp.float32)


def product_kernel(block, n_pieces, sets_ref, a_ref, mine_ref, other_ref, rows_ref, out_ref, z_ref, w_ref, t_ref):
    piece = mine_ref.shape[1]
    n_blocks = a_ref.shape[0] // block
    core = sets_ref[2 * n_blocks]
    column = sets_ref[2 * n_blocks + 1]
    for g, source in enumerate((mine_ref, other_ref)):
        for z in range(source.shape[0]):
            s = column ^ (2 * z + (core ^ g))
            z_ref[pl.ds(pl.multiple_of(s * piece, 16), piece), :] = source[z]
    for b in range(n_blocks):
        of_second = sets_ref[n_blocks + b].astype(jnp.float32)
        rows = pl.ds(b * block, block)
        z = z_ref[rows, :]
        for k, keep in enumerate((1.0 - of_second, of_second)):
            high, low = split(z * keep)
            w_ref[k, 0, rows, :] = high
            w_ref[k, 1, rows, :] = low
    t_ref[...] = jnp.zeros_like(t_ref)
    for b in range(n_blocks):
        k = sets_ref[b]
        rows = pl.ds(b * block, block)
        a_high, a_low = split(a_ref[rows, :])
        w_high = w_ref[k, 0]
        y = -(dot(a_high, w_high, (1,)) + dot(a_low, w_high, (1,)) + dot(a_high, w_ref[k, 1], (1,)))
        z_ref[rows, :] = y
        y_high, y_low = split(y)
        p_high, p_low = split(rows_ref[rows, :])
        t_ref[k] += dot(p_high, y_high, (0,)) + dot(p_low, y_high, (0,)) + dot(p_high, y_low, (0,))
    per = t_ref.shape[0] * block // n_pieces
    each = block // per
    for s in range(n_pieces):
        out_ref[s, :piece, :] = z_ref[s * piece : (s + 1) * piece, :]
        out_ref[s, piece:, :] = t_ref[s // each, (s % each) * per : (s % each + 1) * per, :]


def per_device(inverse_block, l_panel, d_inverse, owner_map, ancestors):
    block = d_inverse.shape[1]
    rows_dev = l_panel.shape[0]
    n_row = lax.axis_size(ROW)
    n_col = lax.axis_size(COL)
    row = lax.axis_index(ROW)
    col = lax.axis_index(COL)
    core = row % 2
    edge = inverse_block.shape[0]
    n_blocks = edge // block

    second = jnp.any(owner_map[:, None] == ancestors[1][None, :], axis=1).astype(jnp.int32)
    start = (row * n_col + col) * rows_dev
    row_blocks = (start + jnp.arange(rows_dev, dtype=jnp.int32)) // block
    row_second = jnp.any(
        (row_blocks[:, None] == jnp.arange(second.shape[0], dtype=jnp.int32)[None, :]) & (second[None, :] == 1),
        axis=1,
        keepdims=True,
    )
    z = jnp.where(row_second, l_panel[:, block:], l_panel[:, :block])

    z_rows = lax.all_gather(z, COL, axis=0, tiled=True)
    turned = lax.ppermute(
        z, (ROW, COL), [(j * n_col + s, (j ^ s) * n_col + j) for j in range(n_row) for s in range(n_col)]
    )
    groups = [list(range(c, n_row, 2)) for c in range(2)]
    mine = lax.all_gather(turned, ROW, axis=0, axis_index_groups=groups)
    other = lax.ppermute(mine, ROW, [(i, i ^ 1) for i in range(n_row)])

    sets = jnp.concatenate(
        [
            lax.dynamic_slice(second, (row * n_blocks,), (n_blocks,)),
            lax.dynamic_slice(second, (col * n_blocks,), (n_blocks,)),
            jnp.stack([core, col]).astype(jnp.int32),
        ]
    )
    per = 2 * block // n_col
    vmem = pl.BlockSpec(memory_space=pltpu.VMEM)
    sent = pl.pallas_call(
        functools.partial(product_kernel, block, n_col),
        out_shape=jax.ShapeDtypeStruct((n_col, rows_dev + per, block), jnp.float32),
        in_specs=[pl.BlockSpec(memory_space=pltpu.SMEM), vmem, vmem, vmem, vmem],
        out_specs=vmem,
        scratch_shapes=[
            pltpu.VMEM((edge, block), jnp.float32),
            pltpu.VMEM((2, 2, edge, block), jnp.bfloat16),
            pltpu.VMEM((2, block, block), jnp.float32),
        ],
        compiler_params=pltpu.CompilerParams(vmem_limit_bytes=40 * 1024 * 1024),
        cost_estimate=pl.CostEstimate(
            flops=6 * edge * edge * block, bytes_accessed=4 * edge * (edge + 4 * block), transcendentals=0
        ),
    )(sets, inverse_block, mine, other, z_rows)
    summed = jnp.sum(lax.all_to_all(sent, COL, 0, 0), axis=0)

    y = summed[:rows_dev]
    column = jnp.concatenate([jnp.where(row_second, 0.0, y), jnp.where(row_second, y, 0.0)], axis=1)

    half = per // 2
    low, high = summed[rows_dev : rows_dev + half], summed[rows_dev + half :]
    first = core == 0
    terms = jnp.where(first, low, high) + lax.ppermute(
        jnp.where(first, high, low), ROW, [(i, i ^ 1) for i in range(n_row)]
    )
    step = 2
    while step < n_row:
        terms = terms + lax.ppermute(terms, ROW, [(i, i ^ step) for i in range(n_row)])
        step *= 2
    here = lax.all_to_all(jnp.broadcast_to(terms[None], (n_col, half, block)), COL, 0, 0)
    there = lax.ppermute(here, ROW, [(i, i ^ 1) for i in range(n_row)])
    all_terms = jnp.stack([jnp.where(first, here, there), jnp.where(first, there, here)], axis=1)
    return column, d_inverse - all_terms.reshape(2, block, block)


def solution(mesh):
    return jax.shard_map(
        per_device,
        mesh=mesh,
        in_specs=(P(ROW, COL), P((ROW, COL), None), P(), P(), P()),
        out_specs=(P((ROW, COL), None), P()),
        check_vma=False,
    )
```

```python
import functools

import jax
import jax.numpy as jnp
from jax import lax
from jax.experimental import pallas as pl
from jax.experimental.pallas import tpu as pltpu
from jax.sharding import PartitionSpec as P

ROW, COL = "prow", "pcol"


def split(x):
    high = x.astype(jnp.bfloat16)
    low = (x - high.astype(jnp.float32)).astype(jnp.bfloat16)
    return high, low


def dot(a, b, contract):
    return lax.dot_general(a, b, ((contract, (0,)), ((), ())), preferred_element_type=jnp.float32)


def dot3(a, b, contract):
    (a_high, a_low), (b_high, b_low) = a, b
    return dot(a_high, b_high, contract) + dot(a_low, b_high, contract) + dot(a_high, b_low, contract)


def in_second(owner_ref, ancestors_ref, stored):
    number = owner_ref[stored]
    found = jnp.int32(0)
    for a in range(ancestors_ref.shape[1]):
        found = found | (ancestors_ref[1, a] == number).astype(jnp.int32)
    return found


def second_rows(block, n_col, owner_ref, ancestors_ref, shape):
    start = (lax.axis_index(ROW) * n_col + lax.axis_index(COL)) * shape[0]
    first = start // block
    last = (start + shape[0] - 1) // block
    here = start + lax.broadcasted_iota(jnp.int32, shape, 0)
    in_first = in_second(owner_ref, ancestors_ref, first)
    in_last = in_second(owner_ref, ancestors_ref, last)
    return jnp.where(here < (first + 1) * block, in_first, in_last) == 1


def pick_kernel(block, n_col, owner_ref, ancestors_ref, panel_ref, z_ref):
    second = second_rows(block, n_col, owner_ref, ancestors_ref, z_ref.shape)
    z_ref[...] = jnp.where(second, panel_ref[:, block:], panel_ref[:, :block])


def split_kernel(owner_ref, ancestors_ref, a_ref, high_ref, low_ref, sets_ref):
    n = pl.num_programs(0)
    b = pl.program_id(0)
    sets_ref[b] = in_second(owner_ref, ancestors_ref, lax.axis_index(ROW) * n + b)
    sets_ref[n + b] = in_second(owner_ref, ancestors_ref, lax.axis_index(COL) * n + b)
    high_ref[...], low_ref[...] = split(a_ref[...])


def product_kernel(block, sets_ref, high_ref, low_ref, *refs):
    *sources, out_ref, z_ref, w_ref = refs
    piece = out_ref.shape[1]
    n_blocks = high_ref.shape[0] // block
    n_z = out_ref.shape[0] // 2
    row = lax.axis_index(ROW)
    core = row % 2
    column = lax.axis_index(COL)
    steps = [0, 1, 2, 3, 4, 1, 2, 3, 4]
    for n, (source, step) in enumerate(zip(sources, steps)):
        owner = core if n < 5 else 1 - core
        z = (row // 2 + n_z + step * (2 * owner - 1)) % n_z
        for h in range(source.shape[0] // piece):
            s = column ^ (2 * z + (owner ^ h))
            z_ref[pl.ds(pl.multiple_of(s * piece, 16), piece), :] = source[h * piece : (h + 1) * piece, :]
    for b in range(n_blocks):
        of_second = sets_ref[n_blocks + b].astype(jnp.float32)
        rows = pl.ds(b * block, block)
        z = z_ref[rows, :]
        for k, keep in enumerate((1.0 - of_second, of_second)):
            w_ref[k, 0, rows, :], w_ref[k, 1, rows, :] = split(z * keep)
    for b in range(n_blocks):
        k = sets_ref[b]
        rows = pl.ds(b * block, block)
        z_ref[rows, :] = -dot3((high_ref[rows, :], low_ref[rows, :]), (w_ref[k, 0], w_ref[k, 1]), (1,))
    for s in range(out_ref.shape[0]):
        out_ref[s] = z_ref[s * piece : (s + 1) * piece, :]


def finish_kernel(block, n_col, owner_ref, ancestors_ref, parts_ref, z_ref, column_ref, keep_ref, send_ref):
    y = parts_ref[0]
    for s in range(1, parts_ref.shape[0]):
        y = y + parts_ref[s]
    second = second_rows(block, n_col, owner_ref, ancestors_ref, y.shape)
    column_ref[:, :block] = jnp.where(second, 0.0, y)
    column_ref[:, block:] = jnp.where(second, y, 0.0)
    z = z_ref[...]
    kept = second == (lax.axis_index(ROW) % 2 == 1)
    y = split(y)
    keep_ref[...] = dot3(split(jnp.where(kept, z, 0.0)), y, (0,))
    send_ref[...] = dot3(split(jnp.where(kept, 0.0, z)), y, (0,))


def per_device(inverse_block, l_panel, d_inverse, owner_map, ancestors):
    block = d_inverse.shape[1]
    rows_dev = l_panel.shape[0]
    n_row = lax.axis_size(ROW)
    n_col = lax.axis_size(COL)
    edge = inverse_block.shape[0]
    n_blocks = edge // block
    n_z = n_row // 2
    f32 = jnp.float32
    smem = pl.BlockSpec(memory_space=pltpu.SMEM)
    vmem = pl.BlockSpec(memory_space=pltpu.VMEM)
    limit = lambda mib: mib * 1024 * 1024
    swap = [(i, i ^ 1) for i in range(n_row)]
    groups = [list(range(c, n_row, 2)) for c in range(2)]

    z = pl.pallas_call(
        functools.partial(pick_kernel, block, n_col),
        out_shape=jax.ShapeDtypeStruct((rows_dev, block), f32),
        in_specs=[smem, smem, vmem],
        out_specs=vmem,
        compiler_params=pltpu.CompilerParams(vmem_limit_bytes=limit(4)),
    )(owner_map, ancestors, l_panel)
    turned = lax.ppermute(
        z, (ROW, COL), [(j * n_col + s, (j ^ s) * n_col + j) for j in range(n_row) for s in range(n_col)]
    )
    strip = pl.BlockSpec((block, edge), lambda b: (b, 0))
    high, low, sets = pl.pallas_call(
        split_kernel,
        grid=(n_blocks,),
        out_shape=[
            jax.ShapeDtypeStruct((edge, edge), jnp.bfloat16),
            jax.ShapeDtypeStruct((edge, edge), jnp.bfloat16),
            jax.ShapeDtypeStruct((2 * n_blocks,), jnp.int32),
        ],
        in_specs=[smem, smem, strip],
        out_specs=[strip, strip, smem],
        compiler_params=pltpu.CompilerParams(vmem_limit_bytes=limit(16)),
        cost_estimate=pl.CostEstimate(flops=4 * edge * edge, bytes_accessed=8 * edge * edge, transcendentals=0),
    )(owner_map, ancestors, inverse_block)
    turned, high, low, sets = lax.optimization_barrier((turned, high, low, sets))

    def along(x, step):
        pairs = [(2 * q + c, 2 * ((q + step * (1 - 2 * c)) % n_z) + c) for q in range(n_z) for c in range(2)]
        return lax.ppermute(x, ROW, pairs)

    chunk = jnp.concatenate([turned, lax.ppermute(turned, ROW, swap)])
    one, two = along(chunk, 1), along(chunk, 2)
    three, four = along(two, 1), along(two[:rows_dev], 2)
    pieces = [one, two, three, four]
    pieces = [chunk, *pieces, *(lax.ppermute(p, ROW, swap) for p in pieces)]

    sent = pl.pallas_call(
        functools.partial(product_kernel, block),
        out_shape=jax.ShapeDtypeStruct((n_col, rows_dev, block), f32),
        in_specs=[smem, vmem, vmem] + [vmem] * len(pieces),
        out_specs=vmem,
        scratch_shapes=[pltpu.VMEM((edge, block), f32), pltpu.VMEM((2, 2, edge, block), jnp.bfloat16)],
        compiler_params=pltpu.CompilerParams(vmem_limit_bytes=limit(20)),
        cost_estimate=pl.CostEstimate(
            flops=6 * edge * edge * block, bytes_accessed=4 * edge * (edge + 2 * block), transcendentals=0
        ),
    )(sets, high, low, *pieces)
    parts = lax.all_to_all(sent, COL, 0, 0)

    column, keep, send = pl.pallas_call(
        functools.partial(finish_kernel, block, n_col),
        out_shape=[
            jax.ShapeDtypeStruct((rows_dev, 2 * block), f32),
            jax.ShapeDtypeStruct((block, block), f32),
            jax.ShapeDtypeStruct((block, block), f32),
        ],
        in_specs=[smem, smem, vmem, vmem],
        out_specs=[vmem, vmem, vmem],
        compiler_params=pltpu.CompilerParams(vmem_limit_bytes=limit(12)),
    )(owner_map, ancestors, parts, z)

    per = block // n_col
    terms = keep + lax.ppermute(send, ROW, swap)
    terms = jnp.sum(lax.all_to_all(terms.reshape(n_col, per, block), COL, 0, 0), axis=0)
    terms = jnp.broadcast_to(terms[None], (n_z, per, block))
    terms = jnp.sum(lax.all_to_all(terms, ROW, 0, 0, axis_index_groups=groups), axis=0)
    terms = jnp.broadcast_to(terms[None], (n_col, per, block))
    here = lax.all_to_all(terms, COL, 0, 0).reshape(block, block)
    there = lax.ppermute(here, ROW, swap)
    first = lax.axis_index(ROW) % 2 == 0
    diag = d_inverse - jnp.stack([jnp.where(first, here, there), jnp.where(first, there, here)])
    return column, diag


def solution(mesh):
    return jax.shard_map(
        per_device,
        mesh=mesh,
        in_specs=(P(ROW, COL), P((ROW, COL), None), P(), P(), P()),
        out_specs=(P((ROW, COL), None), P()),
        check_vma=False,
    )
```

```python
import functools

import jax
import jax.numpy as jnp
from jax import lax
from jax.experimental import pallas as pl
from jax.experimental.pallas import tpu as pltpu
from jax.sharding import PartitionSpec as P

ROW, COL = "prow", "pcol"


def placement(n_row, n_col):
    side = 1
    while side * side < n_col:
        side *= 2
    n_z = n_row // 2
    ring = lambda n, d: min(d % n, -d % n)
    offsets = sorted(range(n_col), key=lambda o: -(ring(side, o // side) + ring(n_col // side, o % side)))
    planes = sorted(range(n_z), key=lambda q: ring(n_z, q))
    table = [0] * n_row
    for n, offset in enumerate(offsets):
        table[2 * planes[n // 2] + n % 2] = offset
    return side, table


def source_of(column, offset, side, n_col):
    wide = n_col // side
    return (column // wide + offset // wide) % side * wide + (column + offset) % wide


def split(x):
    high = x.astype(jnp.bfloat16)
    low = (x - high.astype(jnp.float32)).astype(jnp.bfloat16)
    return high, low


def dot(a, b, contract):
    return lax.dot_general(a, b, ((contract, (0,)), ((), ())), preferred_element_type=jnp.float32)


def dot3(a, b, contract):
    (a_high, a_low), (b_high, b_low) = a, b
    return dot(a_high, b_high, contract) + dot(a_low, b_high, contract) + dot(a_high, b_low, contract)


def in_second(owner_ref, ancestors_ref, stored):
    number = owner_ref[stored]
    found = jnp.int32(0)
    for a in range(ancestors_ref.shape[1]):
        found = found | (ancestors_ref[1, a] == number).astype(jnp.int32)
    return found


def second_rows(block, start, shape, in_first, in_last):
    bound = (start // block + 1) * block - start
    return jnp.where(lax.broadcasted_iota(jnp.int32, shape, 0) < bound, in_first, in_last) == 1


def fetch(pairs, sems):
    copies = [pltpu.make_async_copy(*pair, sems.at[n]) for n, pair in enumerate(pairs)]
    for copy in copies:
        copy.start()
    return copies


def pick_kernel(block, n_col, owner_hbm, ancestors_hbm, panel_hbm, z_ref, owner_ref, ancestors_ref, panel_ref, sems):
    for copy in fetch([(owner_hbm, owner_ref), (ancestors_hbm, ancestors_ref), (panel_hbm, panel_ref)], sems):
        copy.wait()
    rows = z_ref.shape[0]
    start = (lax.axis_index(ROW) * n_col + lax.axis_index(COL)) * rows
    in_first = in_second(owner_ref, ancestors_ref, start // block)
    in_last = in_second(owner_ref, ancestors_ref, (start + rows - 1) // block)
    second = second_rows(block, start, z_ref.shape, in_first, in_last)
    z_ref[...] = jnp.where(second, panel_ref[:, block:], panel_ref[:, :block])


def split_kernel(block, n_col, rows_dev, place, owner_hbm, ancestors_hbm, a_hbm, high_ref, low_ref, sets_ref, owner_ref, ancestors_ref, a_ref, sems):
    n = a_hbm.shape[0] // block
    strips = [pl.ds(b * block, block) for b in range(n)]
    pairs = [(owner_hbm, owner_ref), (ancestors_hbm, ancestors_ref)] + [(a_hbm.at[rows], a_ref.at[rows]) for rows in strips]
    copies = fetch(pairs, sems)
    copies[0].wait()
    copies[1].wait()
    row, col = lax.axis_index(ROW), lax.axis_index(COL)
    start = (row * n_col + col) * rows_dev
    stored = [row * n + b for b in range(n)] + [col * n + b for b in range(n)]
    stored += [start // block, (start + rows_dev - 1) // block]
    for at, which in enumerate(stored):
        sets_ref[at] = in_second(owner_ref, ancestors_ref, which)
    side, table = place
    n_row = len(table)
    for relative, offset in enumerate(table):
        sets_ref[2 * n + 2 + (col // 2 * 2 + relative) % n_row] = source_of(col, offset, side, n_col)
    for copy, rows in zip(copies[2:], strips):
        copy.wait()
        high_ref[rows, :], low_ref[rows, :] = split(a_ref[rows, :])


def product_kernel(block, piece, n_z, sets_ref, high_ref, low_ref, *refs):
    *sources, out_ref, w_ref = refs
    n_blocks = high_ref.shape[0] // block
    row = lax.axis_index(ROW)
    core = row % 2
    steps = [0, 1, 2, 3, 4, 1, 2, 3, 4]
    for n, (source, step) in enumerate(zip(sources, steps)):
        owner = core if n < 5 else 1 - core
        z = (row // 2 + n_z + step * (2 * owner - 1)) % n_z
        for h in range(source.shape[0] // piece):
            start = sets_ref[2 * n_blocks + 2 + 2 * z + (owner ^ h)] * piece
            rows = pl.ds(pl.multiple_of(start, 16), piece)
            in_first = sets_ref[n_blocks + start // block]
            in_last = sets_ref[n_blocks + (start + piece - 1) // block]
            second = second_rows(block, start, (piece, block), in_first, in_last)
            values = source[h * piece : (h + 1) * piece, :]
            for k, kept in enumerate((jnp.where(second, 0.0, values), jnp.where(second, values, 0.0))):
                w_ref[k, 0, rows, :], w_ref[k, 1, rows, :] = split(kept)
    for b in range(n_blocks):
        k = sets_ref[b]
        rows = pl.ds(b * block, block)
        out_ref[rows, :] = -dot3((high_ref[rows, :], low_ref[rows, :]), (w_ref[k, 0], w_ref[k, 1]), (1,))


def finish_kernel(block, n_col, n_blocks, sets_ref, parts_ref, z_ref, column_ref, keep_ref, send_ref):
    y = parts_ref[0]
    for s in range(1, parts_ref.shape[0]):
        y = y + parts_ref[s]
    start = (lax.axis_index(ROW) * n_col + lax.axis_index(COL)) * y.shape[0]
    second = second_rows(block, start, y.shape, sets_ref[2 * n_blocks], sets_ref[2 * n_blocks + 1])
    column_ref[:, :block] = jnp.where(second, 0.0, y)
    column_ref[:, block:] = jnp.where(second, y, 0.0)
    z = z_ref[...]
    kept = second == (lax.axis_index(ROW) % 2 == 1)
    y = split(y)
    keep_ref[...] = dot3(split(jnp.where(kept, z, 0.0)), y, (0,))
    send_ref[...] = dot3(split(jnp.where(kept, 0.0, z)), y, (0,))


def per_device(inverse_block, l_panel, d_inverse, owner_map, ancestors):
    block = d_inverse.shape[1]
    rows_dev = l_panel.shape[0]
    n_row = lax.axis_size(ROW)
    n_col = lax.axis_size(COL)
    edge = inverse_block.shape[0]
    n_blocks = edge // block
    n_z = n_row // 2
    f32 = jnp.float32
    smem = pl.BlockSpec(memory_space=pltpu.SMEM)
    vmem = pl.BlockSpec(memory_space=pltpu.VMEM)
    limit = lambda mib: mib * 1024 * 1024
    swap = [(i, i ^ 1) for i in range(n_row)]
    groups = [list(range(c, n_row, 2)) for c in range(2)]

    hbm = pl.BlockSpec(memory_space=pltpu.HBM)
    small = [
        pltpu.SMEM(owner_map.shape, jnp.int32),
        pltpu.SMEM(ancestors.shape, jnp.int32),
    ]
    z = pl.pallas_call(
        functools.partial(pick_kernel, block, n_col),
        out_shape=jax.ShapeDtypeStruct((rows_dev, block), f32),
        in_specs=[hbm, hbm, hbm],
        out_specs=vmem,
        scratch_shapes=[*small, pltpu.VMEM(l_panel.shape, f32), pltpu.SemaphoreType.DMA((3,))],
        compiler_params=pltpu.CompilerParams(vmem_limit_bytes=limit(60)),
    )(owner_map, ancestors, l_panel)
    side, table = place = placement(n_row, n_col)
    targets = {}
    for j in range(n_row):
        for relative, offset in enumerate(table):
            targets[j, source_of(j, offset, side, n_col)] = (j // 2 * 2 + relative) % n_row
    turned = lax.ppermute(z, (ROW, COL), [(j * n_col + s, p * n_col + j) for (j, s), p in targets.items()])
    high, low, sets = pl.pallas_call(
        functools.partial(split_kernel, block, n_col, rows_dev, place),
        out_shape=[
            jax.ShapeDtypeStruct((edge, edge), jnp.bfloat16),
            jax.ShapeDtypeStruct((edge, edge), jnp.bfloat16),
            jax.ShapeDtypeStruct((2 * n_blocks + 2 + n_row,), jnp.int32),
        ],
        in_specs=[hbm, hbm, hbm],
        out_specs=[vmem, vmem, smem],
        scratch_shapes=[*small, pltpu.VMEM((edge, edge), f32), pltpu.SemaphoreType.DMA((n_blocks + 2,))],
        compiler_params=pltpu.CompilerParams(vmem_limit_bytes=limit(44)),
        cost_estimate=pl.CostEstimate(flops=4 * edge * edge, bytes_accessed=8 * edge * edge, transcendentals=0),
    )(owner_map, ancestors, inverse_block)
    turned, high, low, sets = lax.optimization_barrier((turned, high, low, sets))

    def along(x, step):
        pairs = [(2 * q + c, 2 * ((q + step * (1 - 2 * c)) % n_z) + c) for q in range(n_z) for c in range(2)]
        return lax.ppermute(x, ROW, pairs)

    chunk = jnp.concatenate([turned, lax.ppermute(turned, ROW, swap)])
    one, two = along(chunk, 1), along(chunk, 2)
    three, four = along(two, 1), along(two[:rows_dev], 2)
    pieces = [one, two, three, four]
    pieces = [chunk, *pieces, *(lax.ppermute(p, ROW, swap) for p in pieces)]

    sent = pl.pallas_call(
        functools.partial(product_kernel, block, rows_dev, n_z),
        out_shape=jax.ShapeDtypeStruct((edge, block), f32),
        in_specs=[smem, vmem, vmem] + [vmem] * len(pieces),
        out_specs=vmem,
        scratch_shapes=[pltpu.VMEM((2, 2, edge, block), jnp.bfloat16)],
        compiler_params=pltpu.CompilerParams(vmem_limit_bytes=limit(20)),
        cost_estimate=pl.CostEstimate(
            flops=6 * edge * edge * block, bytes_accessed=4 * edge * (edge + 2 * block), transcendentals=0
        ),
    )(sets, high, low, *pieces)
    parts = lax.all_to_all(sent.reshape(n_col, rows_dev, block), COL, 0, 0)

    column, keep, send = pl.pallas_call(
        functools.partial(finish_kernel, block, n_col, n_blocks),
        out_shape=[
            jax.ShapeDtypeStruct((rows_dev, 2 * block), f32),
            jax.ShapeDtypeStruct((block, block), f32),
            jax.ShapeDtypeStruct((block, block), f32),
        ],
        in_specs=[smem, vmem, vmem],
        out_specs=[vmem, vmem, vmem],
        compiler_params=pltpu.CompilerParams(vmem_limit_bytes=limit(12)),
    )(sets, parts, z)

    per = block // n_col
    terms = keep + lax.ppermute(send, ROW, swap)
    terms = jnp.sum(lax.all_to_all(terms.reshape(n_col, per, block), COL, 0, 0), axis=0)
    terms = jnp.broadcast_to(terms[None], (n_z, per, block))
    terms = jnp.sum(lax.all_to_all(terms, ROW, 0, 0, axis_index_groups=groups), axis=0)
    terms = jnp.broadcast_to(terms[None], (n_col, per, block))
    here = lax.all_to_all(terms, COL, 0, 0).reshape(block, block)
    there = lax.ppermute(here, ROW, swap)
    first = lax.axis_index(ROW) % 2 == 0
    diag = d_inverse - jnp.stack([jnp.where(first, here, there), jnp.where(first, there, here)])
    return column, diag


def solution(mesh):
    return jax.shard_map(
        per_device,
        mesh=mesh,
        in_specs=(P(ROW, COL), P((ROW, COL), None), P(), P(), P()),
        out_specs=(P((ROW, COL), None), P()),
        check_vma=False,
    )
```

```python
import functools

import jax
import jax.numpy as jnp
from jax import lax
from jax.experimental import pallas as pl
from jax.experimental.pallas import tpu as pltpu
from jax.sharding import PartitionSpec as P

ROW, COL = "prow", "pcol"


def placement(n_row, n_col):
    side = 1
    while side * side < n_col:
        side *= 2
    n_z = n_row // 2
    ring = lambda n, d: min(d % n, -d % n)
    offsets = sorted(range(n_col), key=lambda o: -(ring(side, o // side) + ring(n_col // side, o % side)))
    planes = sorted(range(n_z), key=lambda q: ring(n_z, q))
    table = [0] * n_row
    for n, offset in enumerate(offsets):
        table[2 * planes[n // 2] + n % 2] = offset
    return side, table


def source_of(column, offset, side, n_col):
    wide = n_col // side
    return (column // wide + offset // wide) % side * wide + (column + offset) % wide


def split(x):
    high = x.astype(jnp.bfloat16)
    low = (x - high.astype(jnp.float32)).astype(jnp.bfloat16)
    return high, low


def dot(a, b, contract):
    return lax.dot_general(a, b, ((contract, (0,)), ((), ())), preferred_element_type=jnp.float32)


def dot3(a, b, contract):
    (a_high, a_low), (b_high, b_low) = a, b
    return dot(a_high, b_high, contract) + dot(a_low, b_high, contract) + dot(a_high, b_low, contract)


def in_second(owner_ref, ancestors_ref, stored):
    number = owner_ref[stored]
    found = jnp.int32(0)
    for a in range(ancestors_ref.shape[1]):
        found = found | (ancestors_ref[1, a] == number).astype(jnp.int32)
    return found


def second_rows(block, start, shape, in_first, in_last):
    bound = (start // block + 1) * block - start
    return jnp.where(lax.broadcasted_iota(jnp.int32, shape, 0) < bound, in_first, in_last) == 1


def fetch(pairs, sems):
    copies = [pltpu.make_async_copy(*pair, sems.at[n]) for n, pair in enumerate(pairs)]
    for copy in copies:
        copy.start()
    return copies


def pick_kernel(block, n_col, owner_hbm, ancestors_hbm, panel_hbm, z_ref, owner_ref, ancestors_ref, panel_ref, sems):
    for copy in fetch([(owner_hbm, owner_ref), (ancestors_hbm, ancestors_ref), (panel_hbm, panel_ref)], sems):
        copy.wait()
    rows = z_ref.shape[0]
    start = (lax.axis_index(ROW) * n_col + lax.axis_index(COL)) * rows
    in_first = in_second(owner_ref, ancestors_ref, start // block)
    in_last = in_second(owner_ref, ancestors_ref, (start + rows - 1) // block)
    second = second_rows(block, start, z_ref.shape, in_first, in_last)
    z_ref[...] = jnp.where(second, panel_ref[:, block:], panel_ref[:, :block])


def split_kernel(block, n_col, rows_dev, place, owner_hbm, ancestors_hbm, a_hbm, high_ref, low_ref, sets_ref, owner_ref, ancestors_ref, a_ref, sems):
    n = a_hbm.shape[0] // block
    strips = [pl.ds(b * block, block) for b in range(n)]
    pairs = [(owner_hbm, owner_ref), (ancestors_hbm, ancestors_ref)] + [(a_hbm.at[rows], a_ref.at[rows]) for rows in strips]
    copies = fetch(pairs, sems)
    copies[0].wait()
    copies[1].wait()
    row, col = lax.axis_index(ROW), lax.axis_index(COL)
    start = (row * n_col + col) * rows_dev
    stored = [row * n + b for b in range(n)] + [col * n + b for b in range(n)]
    stored += [start // block, (start + rows_dev - 1) // block]
    for at, which in enumerate(stored):
        sets_ref[at] = in_second(owner_ref, ancestors_ref, which)
    side, table = place
    n_row = len(table)
    for relative, offset in enumerate(table):
        sets_ref[2 * n + 2 + (col // 2 * 2 + relative) % n_row] = source_of(col, offset, side, n_col)
    for copy, rows in zip(copies[2:], strips):
        copy.wait()
        high_ref[rows, :], low_ref[rows, :] = split(a_ref[rows, :])


def product_kernel(block, piece, n_z, sets_ref, high_ref, low_ref, *refs):
    *sources, out_ref, w_ref = refs
    n_blocks = high_ref.shape[0] // block
    row = lax.axis_index(ROW)
    core = row % 2
    steps = [0, 1, 2, 3, 4, 1, 2, 3, 4]
    for n, (source, step) in enumerate(zip(sources, steps)):
        owner = core if n < 5 else 1 - core
        z = (row // 2 + n_z + step * (2 * owner - 1)) % n_z
        for h in range(source.shape[0] // piece):
            start = sets_ref[2 * n_blocks + 2 + 2 * z + (owner ^ h)] * piece
            rows = pl.ds(pl.multiple_of(start, 16), piece)
            in_first = sets_ref[n_blocks + start // block]
            in_last = sets_ref[n_blocks + (start + piece - 1) // block]
            second = second_rows(block, start, (piece, block), in_first, in_last)
            values = source[h * piece : (h + 1) * piece, :]
            for k, kept in enumerate((jnp.where(second, 0.0, values), jnp.where(second, values, 0.0))):
                w_ref[k, 0, rows, :], w_ref[k, 1, rows, :] = split(kept)
    for b in range(n_blocks):
        k = sets_ref[b]
        rows = pl.ds(b * block, block)
        out_ref[rows, :] = -dot3((high_ref[rows, :], low_ref[rows, :]), (w_ref[k, 0], w_ref[k, 1]), (1,))


def rows_terms(block, n_col, n_blocks, sets_ref, z_ref, y, of_sibling):
    start = (lax.axis_index(ROW) * n_col + lax.axis_index(COL)) * y.shape[0]
    second = second_rows(block, start, y.shape, sets_ref[2 * n_blocks], sets_ref[2 * n_blocks + 1])
    kept = second == ((lax.axis_index(ROW) + of_sibling) % 2 == 1)
    return second, dot3(split(jnp.where(kept, z_ref[...], 0.0)), split(y), (0,))


def send_kernel(block, n_col, n_blocks, sets_ref, parts_ref, z_ref, y_ref, send_ref):
    y = parts_ref[0]
    for s in range(1, parts_ref.shape[0]):
        y = y + parts_ref[s]
    y_ref[...] = y
    send_ref[...] = rows_terms(block, n_col, n_blocks, sets_ref, z_ref, y, 1)[1]


def keep_kernel(block, n_col, n_blocks, sets_ref, y_ref, z_ref, keep_ref):
    keep_ref[...] = rows_terms(block, n_col, n_blocks, sets_ref, z_ref, y_ref[...], 0)[1]


def column_kernel(block, n_col, n_blocks, sets_ref, y_ref, column_ref):
    y = y_ref[...]
    start = (lax.axis_index(ROW) * n_col + lax.axis_index(COL)) * y.shape[0]
    second = second_rows(block, start, y.shape, sets_ref[2 * n_blocks], sets_ref[2 * n_blocks + 1])
    column_ref[:, :block] = jnp.where(second, 0.0, y)
    column_ref[:, block:] = jnp.where(second, y, 0.0)


def last_kernel(d_ref, here_ref, there_ref, out_ref):
    core = lax.axis_index(ROW) % 2
    out_ref[core] = d_ref[core] - here_ref[...]
    out_ref[1 - core] = d_ref[1 - core] - there_ref[...]


def per_device(inverse_block, l_panel, d_inverse, owner_map, ancestors):
    block = d_inverse.shape[1]
    rows_dev = l_panel.shape[0]
    n_row = lax.axis_size(ROW)
    n_col = lax.axis_size(COL)
    edge = inverse_block.shape[0]
    n_blocks = edge // block
    n_z = n_row // 2
    f32 = jnp.float32
    smem = pl.BlockSpec(memory_space=pltpu.SMEM)
    vmem = pl.BlockSpec(memory_space=pltpu.VMEM)
    limit = lambda mib: mib * 1024 * 1024
    swap = [(i, i ^ 1) for i in range(n_row)]
    groups = [list(range(c, n_row, 2)) for c in range(2)]

    hbm = pl.BlockSpec(memory_space=pltpu.HBM)
    small = [
        pltpu.SMEM(owner_map.shape, jnp.int32),
        pltpu.SMEM(ancestors.shape, jnp.int32),
    ]
    z = pl.pallas_call(
        functools.partial(pick_kernel, block, n_col),
        out_shape=jax.ShapeDtypeStruct((rows_dev, block), f32),
        in_specs=[hbm, hbm, hbm],
        out_specs=vmem,
        scratch_shapes=[*small, pltpu.VMEM(l_panel.shape, f32), pltpu.SemaphoreType.DMA((3,))],
        compiler_params=pltpu.CompilerParams(vmem_limit_bytes=limit(60)),
    )(owner_map, ancestors, l_panel)
    side, table = place = placement(n_row, n_col)
    targets = {}
    for j in range(n_row):
        for relative, offset in enumerate(table):
            targets[j, source_of(j, offset, side, n_col)] = (j // 2 * 2 + relative) % n_row
    turned = lax.ppermute(z, (ROW, COL), [(j * n_col + s, p * n_col + j) for (j, s), p in targets.items()])
    high, low, sets = pl.pallas_call(
        functools.partial(split_kernel, block, n_col, rows_dev, place),
        out_shape=[
            jax.ShapeDtypeStruct((edge, edge), jnp.bfloat16),
            jax.ShapeDtypeStruct((edge, edge), jnp.bfloat16),
            jax.ShapeDtypeStruct((2 * n_blocks + 2 + n_row,), jnp.int32),
        ],
        in_specs=[hbm, hbm, hbm],
        out_specs=[vmem, vmem, smem],
        scratch_shapes=[*small, pltpu.VMEM((edge, edge), f32), pltpu.SemaphoreType.DMA((n_blocks + 2,))],
        compiler_params=pltpu.CompilerParams(vmem_limit_bytes=limit(44)),
        cost_estimate=pl.CostEstimate(flops=4 * edge * edge, bytes_accessed=8 * edge * edge, transcendentals=0),
    )(owner_map, ancestors, inverse_block)
    turned, high, low, sets = lax.optimization_barrier((turned, high, low, sets))

    def along(x, step):
        pairs = [(2 * q + c, 2 * ((q + step * (1 - 2 * c)) % n_z) + c) for q in range(n_z) for c in range(2)]
        return lax.ppermute(x, ROW, pairs)

    chunk = jnp.concatenate([turned, lax.ppermute(turned, ROW, swap)])
    one, two = along(chunk, 1), along(chunk, 2)
    three, four = along(two, 1), along(two[:rows_dev], 2)
    pieces = [one, two, three, four]
    pieces = [chunk, *pieces, *(lax.ppermute(p, ROW, swap) for p in pieces)]

    sent = pl.pallas_call(
        functools.partial(product_kernel, block, rows_dev, n_z),
        out_shape=jax.ShapeDtypeStruct((edge, block), f32),
        in_specs=[smem, vmem, vmem] + [vmem] * len(pieces),
        out_specs=vmem,
        scratch_shapes=[pltpu.VMEM((2, 2, edge, block), jnp.bfloat16)],
        compiler_params=pltpu.CompilerParams(vmem_limit_bytes=limit(20)),
        cost_estimate=pl.CostEstimate(
            flops=6 * edge * edge * block, bytes_accessed=4 * edge * (edge + 2 * block), transcendentals=0
        ),
    )(sets, high, low, *pieces)
    parts = lax.all_to_all(sent.reshape(n_col, rows_dev, block), COL, 0, 0)

    square = jax.ShapeDtypeStruct((block, block), f32)
    small_limit = pltpu.CompilerParams(vmem_limit_bytes=limit(12))
    y, send = pl.pallas_call(
        functools.partial(send_kernel, block, n_col, n_blocks),
        out_shape=[jax.ShapeDtypeStruct((rows_dev, block), f32), square],
        in_specs=[smem, vmem, vmem],
        out_specs=[vmem, vmem],
        compiler_params=small_limit,
    )(sets, parts, z)
    keep = pl.pallas_call(
        functools.partial(keep_kernel, block, n_col, n_blocks),
        out_shape=square,
        in_specs=[smem, vmem, vmem],
        out_specs=vmem,
        compiler_params=small_limit,
    )(sets, y, z)

    per = block // n_col
    terms = keep + lax.ppermute(send, ROW, swap)
    terms = jnp.sum(lax.all_to_all(terms.reshape(n_col, per, block), COL, 0, 0), axis=0)
    terms = jnp.broadcast_to(terms[None], (n_z, per, block))
    terms = jnp.sum(lax.all_to_all(terms, ROW, 0, 0, axis_index_groups=groups), axis=0)
    terms = jnp.broadcast_to(terms[None], (n_col, per, block))
    here = lax.all_to_all(terms, COL, 0, 0).reshape(block, block)
    there = lax.ppermute(here, ROW, swap)
    y, here = lax.optimization_barrier((y, here))
    column = pl.pallas_call(
        functools.partial(column_kernel, block, n_col, n_blocks),
        out_shape=jax.ShapeDtypeStruct((rows_dev, 2 * block), f32),
        in_specs=[smem, vmem],
        out_specs=vmem,
        compiler_params=small_limit,
    )(sets, y)
    there, column = lax.optimization_barrier((there, column))
    diag = pl.pallas_call(
        last_kernel,
        out_shape=jax.ShapeDtypeStruct(d_inverse.shape, f32),
        in_specs=[vmem, vmem, vmem],
        out_specs=vmem,
        compiler_params=small_limit,
    )(d_inverse, here, there)
    return column, diag


def solution(mesh):
    return jax.shard_map(
        per_device,
        mesh=mesh,
        in_specs=(P(ROW, COL), P((ROW, COL), None), P(), P(), P()),
        out_specs=(P((ROW, COL), None), P()),
        check_vma=False,
    )
```

```python
import functools

import jax
import jax.numpy as jnp
from jax import lax
from jax.experimental import pallas as pl
from jax.experimental.pallas import tpu as pltpu
from jax.sharding import PartitionSpec as P

ROW, COL = "prow", "pcol"


def placement(n_row, n_col):
    side = 1
    while side * side < n_col:
        side *= 2
    n_z = n_row // 2
    ring = lambda n, d: min(d % n, -d % n)
    offsets = sorted(range(n_col), key=lambda o: -(ring(side, o // side) + ring(n_col // side, o % side)))
    planes = sorted(range(n_z), key=lambda q: ring(n_z, q))
    table = [0] * n_row
    for n, offset in enumerate(offsets):
        table[2 * planes[n // 2] + n % 2] = offset
    return side, table


def source_of(column, offset, side, n_col):
    wide = n_col // side
    return (column // wide + offset // wide) % side * wide + (column + offset) % wide


def split(x):
    high = x.astype(jnp.bfloat16)
    low = (x - high.astype(jnp.float32)).astype(jnp.bfloat16)
    return high, low


def dot(a, b, contract):
    return lax.dot_general(a, b, ((contract, (0,)), ((), ())), preferred_element_type=jnp.float32)


def dot3(a, b, contract):
    (a_high, a_low), (b_high, b_low) = a, b
    return dot(a_high, b_high, contract) + dot(a_low, b_high, contract) + dot(a_high, b_low, contract)


def in_second(owner_ref, ancestors_ref, stored):
    number = owner_ref[stored]
    found = jnp.int32(0)
    for a in range(ancestors_ref.shape[1]):
        found = found | (ancestors_ref[1, a] == number).astype(jnp.int32)
    return found


def second_rows(block, start, shape, in_first, in_last):
    bound = (start // block + 1) * block - start
    return jnp.where(lax.broadcasted_iota(jnp.int32, shape, 0) < bound, in_first, in_last) == 1


def fetch(pairs, sems):
    copies = [pltpu.make_async_copy(*pair, sems.at[n]) for n, pair in enumerate(pairs)]
    for copy in copies:
        copy.start()
    return copies


def pick_kernel(block, n_col, owner_hbm, ancestors_hbm, panel_hbm, z_ref, owner_ref, ancestors_ref, panel_ref, sems):
    for copy in fetch([(owner_hbm, owner_ref), (ancestors_hbm, ancestors_ref), (panel_hbm, panel_ref)], sems):
        copy.wait()
    rows = z_ref.shape[0]
    start = (lax.axis_index(ROW) * n_col + lax.axis_index(COL)) * rows
    in_first = in_second(owner_ref, ancestors_ref, start // block)
    in_last = in_second(owner_ref, ancestors_ref, (start + rows - 1) // block)
    second = second_rows(block, start, z_ref.shape, in_first, in_last)
    z_ref[...] = jnp.where(second, panel_ref[:, block:], panel_ref[:, :block])


def split_kernel(block, n_col, rows_dev, place, owner_hbm, ancestors_hbm, a_hbm, high_ref, low_ref, sets_ref, owner_ref, ancestors_ref, a_ref, sems):
    n = a_hbm.shape[0] // block
    strips = [pl.ds(b * block, block) for b in range(n)]
    pairs = [(owner_hbm, owner_ref), (ancestors_hbm, ancestors_ref)] + [(a_hbm.at[rows], a_ref.at[rows]) for rows in strips]
    copies = fetch(pairs, sems)
    copies[0].wait()
    copies[1].wait()
    row, col = lax.axis_index(ROW), lax.axis_index(COL)
    start = (row * n_col + col) * rows_dev
    stored = [row * n + b for b in range(n)] + [col * n + b for b in range(n)]
    stored += [start // block, (start + rows_dev - 1) // block]
    for at, which in enumerate(stored):
        sets_ref[at] = in_second(owner_ref, ancestors_ref, which)
    side, table = place
    n_row = len(table)
    for relative, offset in enumerate(table):
        sets_ref[2 * n + 2 + (col // 2 * 2 + relative) % n_row] = source_of(col, offset, side, n_col)
    for copy, rows in zip(copies[2:], strips):
        copy.wait()
        high_ref[rows, :], low_ref[rows, :] = split(a_ref[rows, :])


def product_kernel(block, piece, n_z, sets_ref, high_ref, low_ref, *refs):
    *sources, out_ref, w_ref = refs
    n_blocks = high_ref.shape[0] // block
    row = lax.axis_index(ROW)
    core = row % 2
    steps = [0, 1, 2, 3, 4, 1, 2, 3]
    for n, (source, step) in enumerate(zip(sources, steps)):
        owner = core if n < 5 else 1 - core
        z = (row // 2 + n_z + step * (2 * owner - 1)) % n_z
        for h in range(source.shape[0] // piece):
            start = sets_ref[2 * n_blocks + 2 + 2 * z + (owner ^ h)] * piece
            rows = pl.ds(pl.multiple_of(start, 16), piece)
            in_first = sets_ref[n_blocks + start // block]
            in_last = sets_ref[n_blocks + (start + piece - 1) // block]
            second = second_rows(block, start, (piece, block), in_first, in_last)
            values = source[h * piece : (h + 1) * piece, :]
            for k, kept in enumerate((jnp.where(second, 0.0, values), jnp.where(second, values, 0.0))):
                w_ref[k, 0, rows, :], w_ref[k, 1, rows, :] = split(kept)
    for b in range(n_blocks):
        k = sets_ref[b]
        rows = pl.ds(b * block, block)
        out_ref[rows, :] = -dot3((high_ref[rows, :], low_ref[rows, :]), (w_ref[k, 0], w_ref[k, 1]), (1,))


def rows_terms(block, n_col, n_blocks, sets_ref, z_ref, y, of_sibling):
    start = (lax.axis_index(ROW) * n_col + lax.axis_index(COL)) * y.shape[0]
    second = second_rows(block, start, y.shape, sets_ref[2 * n_blocks], sets_ref[2 * n_blocks + 1])
    kept = second == ((lax.axis_index(ROW) + of_sibling) % 2 == 1)
    return second, dot3(split(jnp.where(kept, z_ref[...], 0.0)), split(y), (0,))


def send_kernel(block, n_col, n_blocks, sets_ref, parts_ref, z_ref, y_ref, send_ref):
    y = parts_ref[0]
    for s in range(1, parts_ref.shape[0]):
        y = y + parts_ref[s]
    y_ref[...] = y
    send_ref[...] = rows_terms(block, n_col, n_blocks, sets_ref, z_ref, y, 1)[1]


def keep_kernel(block, n_col, n_blocks, sets_ref, y_ref, z_ref, keep_ref):
    keep_ref[...] = rows_terms(block, n_col, n_blocks, sets_ref, z_ref, y_ref[...], 0)[1]


def column_kernel(block, n_col, n_blocks, sets_ref, y_ref, column_ref):
    y = y_ref[...]
    start = (lax.axis_index(ROW) * n_col + lax.axis_index(COL)) * y.shape[0]
    second = second_rows(block, start, y.shape, sets_ref[2 * n_blocks], sets_ref[2 * n_blocks + 1])
    column_ref[:, :block] = jnp.where(second, 0.0, y)
    column_ref[:, block:] = jnp.where(second, y, 0.0)


def last_kernel(d_ref, here_ref, there_ref, out_ref):
    core = lax.axis_index(ROW) % 2
    out_ref[core] = d_ref[core] - here_ref[...]
    out_ref[1 - core] = d_ref[1 - core] - there_ref[...]


def per_device(inverse_block, l_panel, d_inverse, owner_map, ancestors):
    block = d_inverse.shape[1]
    rows_dev = l_panel.shape[0]
    n_row = lax.axis_size(ROW)
    n_col = lax.axis_size(COL)
    edge = inverse_block.shape[0]
    n_blocks = edge // block
    n_z = n_row // 2
    f32 = jnp.float32
    smem = pl.BlockSpec(memory_space=pltpu.SMEM)
    vmem = pl.BlockSpec(memory_space=pltpu.VMEM)
    limit = lambda mib: mib * 1024 * 1024
    swap = [(i, i ^ 1) for i in range(n_row)]
    groups = [list(range(c, n_row, 2)) for c in range(2)]

    hbm = pl.BlockSpec(memory_space=pltpu.HBM)
    small = [
        pltpu.SMEM(owner_map.shape, jnp.int32),
        pltpu.SMEM(ancestors.shape, jnp.int32),
    ]
    z = pl.pallas_call(
        functools.partial(pick_kernel, block, n_col),
        out_shape=jax.ShapeDtypeStruct((rows_dev, block), f32),
        in_specs=[hbm, hbm, hbm],
        out_specs=vmem,
        scratch_shapes=[*small, pltpu.VMEM(l_panel.shape, f32), pltpu.SemaphoreType.DMA((3,))],
        compiler_params=pltpu.CompilerParams(vmem_limit_bytes=limit(60)),
    )(owner_map, ancestors, l_panel)
    side, table = place = placement(n_row, n_col)
    targets = {}
    for j in range(n_row):
        for relative, offset in enumerate(table):
            targets[j, source_of(j, offset, side, n_col)] = (j // 2 * 2 + relative) % n_row
    turned = lax.ppermute(z, (ROW, COL), [(j * n_col + s, p * n_col + j) for (j, s), p in targets.items()])
    high, low, sets = pl.pallas_call(
        functools.partial(split_kernel, block, n_col, rows_dev, place),
        out_shape=[
            jax.ShapeDtypeStruct((edge, edge), jnp.bfloat16),
            jax.ShapeDtypeStruct((edge, edge), jnp.bfloat16),
            jax.ShapeDtypeStruct((2 * n_blocks + 2 + n_row,), jnp.int32),
        ],
        in_specs=[hbm, hbm, hbm],
        out_specs=[vmem, vmem, smem],
        scratch_shapes=[*small, pltpu.VMEM((edge, edge), f32), pltpu.SemaphoreType.DMA((n_blocks + 2,))],
        compiler_params=pltpu.CompilerParams(vmem_limit_bytes=limit(44)),
        cost_estimate=pl.CostEstimate(flops=4 * edge * edge, bytes_accessed=8 * edge * edge, transcendentals=0),
    )(owner_map, ancestors, inverse_block)
    turned, high, low, sets = lax.optimization_barrier((turned, high, low, sets))

    def along(x, step):
        pairs = [(2 * q + c, 2 * ((q + step * (1 - 2 * c)) % n_z) + c) for q in range(n_z) for c in range(2)]
        return lax.ppermute(x, ROW, pairs)

    chunk = jnp.concatenate([turned, lax.ppermute(turned, ROW, swap)])
    one, two = along(chunk, 1), along(chunk, 2)
    three, four = along(two, 1), along(two, 2)
    pieces = [one, two, three]
    pieces = [chunk, *pieces, four, *(lax.ppermute(p, ROW, swap) for p in pieces)]

    sent = pl.pallas_call(
        functools.partial(product_kernel, block, rows_dev, n_z),
        out_shape=jax.ShapeDtypeStruct((edge, block), f32),
        in_specs=[smem, vmem, vmem] + [vmem] * len(pieces),
        out_specs=vmem,
        scratch_shapes=[pltpu.VMEM((2, 2, edge, block), jnp.bfloat16)],
        compiler_params=pltpu.CompilerParams(vmem_limit_bytes=limit(20)),
        cost_estimate=pl.CostEstimate(
            flops=6 * edge * edge * block, bytes_accessed=4 * edge * (edge + 2 * block), transcendentals=0
        ),
    )(sets, high, low, *pieces)
    parts = lax.all_to_all(sent.reshape(n_col, rows_dev, block), COL, 0, 0)

    square = jax.ShapeDtypeStruct((block, block), f32)
    small_limit = pltpu.CompilerParams(vmem_limit_bytes=limit(12))
    y, send = pl.pallas_call(
        functools.partial(send_kernel, block, n_col, n_blocks),
        out_shape=[jax.ShapeDtypeStruct((rows_dev, block), f32), square],
        in_specs=[smem, vmem, vmem],
        out_specs=[vmem, vmem],
        compiler_params=small_limit,
    )(sets, parts, z)
    keep = pl.pallas_call(
        functools.partial(keep_kernel, block, n_col, n_blocks),
        out_shape=square,
        in_specs=[smem, vmem, vmem],
        out_specs=vmem,
        compiler_params=small_limit,
    )(sets, y, z)

    per = block // n_col
    terms = keep + lax.ppermute(send, ROW, swap)
    terms = jnp.sum(lax.all_to_all(terms.reshape(n_col, per, block), COL, 0, 0), axis=0)
    terms = jnp.broadcast_to(terms[None], (n_z, per, block))
    terms = jnp.sum(lax.all_to_all(terms, ROW, 0, 0, axis_index_groups=groups), axis=0)
    terms = jnp.broadcast_to(terms[None], (n_col, per, block))
    here = lax.all_to_all(terms, COL, 0, 0).reshape(block, block)
    there = lax.ppermute(here, ROW, swap)
    y, here = lax.optimization_barrier((y, here))
    column = pl.pallas_call(
        functools.partial(column_kernel, block, n_col, n_blocks),
        out_shape=jax.ShapeDtypeStruct((rows_dev, 2 * block), f32),
        in_specs=[smem, vmem],
        out_specs=vmem,
        compiler_params=small_limit,
    )(sets, y)
    there, column = lax.optimization_barrier((there, column))
    diag = pl.pallas_call(
        last_kernel,
        out_shape=jax.ShapeDtypeStruct(d_inverse.shape, f32),
        in_specs=[vmem, vmem, vmem],
        out_specs=vmem,
        compiler_params=small_limit,
    )(d_inverse, here, there)
    return column, diag


def solution(mesh):
    return jax.shard_map(
        per_device,
        mesh=mesh,
        in_specs=(P(ROW, COL), P((ROW, COL), None), P(), P(), P()),
        out_specs=(P((ROW, COL), None), P()),
        check_vma=False,
    )
```

```python
import functools

import jax
import jax.numpy as jnp
from jax import lax
from jax.experimental import pallas as pl
from jax.experimental.pallas import tpu as pltpu
from jax.sharding import PartitionSpec as P

ROW, COL = "prow", "pcol"


def placement(n_row, n_col):
    side = 1
    while side * side < n_col:
        side *= 2
    n_z = n_row // 2
    ring = lambda n, d: min(d % n, -d % n)
    offsets = sorted(range(n_col), key=lambda o: -(ring(side, o // side) + ring(n_col // side, o % side)))
    planes = sorted(range(n_z), key=lambda q: ring(n_z, q))
    table = [0] * n_row
    for n, offset in enumerate(offsets):
        table[2 * planes[n // 2] + n % 2] = offset
    return side, table


def source_of(column, offset, side, n_col):
    wide = n_col // side
    return (column // wide + offset // wide) % side * wide + (column + offset) % wide


def split(x):
    high = x.astype(jnp.bfloat16)
    low = (x - high.astype(jnp.float32)).astype(jnp.bfloat16)
    return high, low


def dot(a, b, contract):
    return lax.dot_general(a, b, ((contract, (0,)), ((), ())), preferred_element_type=jnp.float32)


def dot3(a, b, contract):
    (a_high, a_low), (b_high, b_low) = a, b
    return dot(a_high, b_high, contract) + dot(a_low, b_high, contract) + dot(a_high, b_low, contract)


def in_second(owner_ref, ancestors_ref, stored):
    number = owner_ref[stored]
    found = jnp.int32(0)
    for a in range(ancestors_ref.shape[1]):
        found = found | (ancestors_ref[1, a] == number).astype(jnp.int32)
    return found


def second_rows(block, start, shape, in_first, in_last):
    bound = (start // block + 1) * block - start
    return jnp.where(lax.broadcasted_iota(jnp.int32, shape, 0) < bound, in_first, in_last) == 1


def fetch(pairs, sems):
    copies = [pltpu.make_async_copy(*pair, sems.at[n]) for n, pair in enumerate(pairs)]
    for copy in copies:
        copy.start()
    return copies


def pick_kernel(block, n_col, owner_hbm, ancestors_hbm, panel_hbm, z_ref, owner_ref, ancestors_ref, panel_ref, sems):
    for copy in fetch([(owner_hbm, owner_ref), (ancestors_hbm, ancestors_ref), (panel_hbm, panel_ref)], sems):
        copy.wait()
    rows = z_ref.shape[0]
    start = (lax.axis_index(ROW) * n_col + lax.axis_index(COL)) * rows
    in_first = in_second(owner_ref, ancestors_ref, start // block)
    in_last = in_second(owner_ref, ancestors_ref, (start + rows - 1) // block)
    second = second_rows(block, start, z_ref.shape, in_first, in_last)
    z_ref[...] = jnp.where(second, panel_ref[:, block:], panel_ref[:, :block])


def split_kernel(block, n_col, rows_dev, place, owner_hbm, ancestors_hbm, a_hbm, high_ref, low_ref, sets_ref, owner_ref, ancestors_ref, a_ref, sems):
    n = a_hbm.shape[0] // block
    strips = [pl.ds(b * block, block) for b in range(n)]
    pairs = [(owner_hbm, owner_ref), (ancestors_hbm, ancestors_ref)] + [(a_hbm.at[rows], a_ref.at[rows]) for rows in strips]
    copies = fetch(pairs, sems)
    copies[0].wait()
    copies[1].wait()
    row, col = lax.axis_index(ROW), lax.axis_index(COL)
    start = (row * n_col + col) * rows_dev
    stored = [row * n + b for b in range(n)] + [col * n + b for b in range(n)]
    stored += [start // block, (start + rows_dev - 1) // block]
    for at, which in enumerate(stored):
        sets_ref[at] = in_second(owner_ref, ancestors_ref, which)
    side, table = place
    n_row = len(table)
    for relative, offset in enumerate(table):
        sets_ref[2 * n + 2 + (col // 2 * 2 + relative) % n_row] = source_of(col, offset, side, n_col)
    for copy, rows in zip(copies[2:], strips):
        copy.wait()
        high_ref[rows, :], low_ref[rows, :] = split(a_ref[rows, :])


def product_kernel(block, piece, n_z, places, sets_ref, high_ref, low_ref, *refs):
    *sources, out_ref, w_ref = refs
    n_blocks = high_ref.shape[0] // block
    row = lax.axis_index(ROW)
    core = row % 2
    for source, (theirs, held) in zip(sources, places):
        owner = 1 - core if theirs else core
        for h, (step, which) in enumerate(held):
            z = (row // 2 + n_z + step * (2 * owner - 1)) % n_z
            start = sets_ref[2 * n_blocks + 2 + 2 * z + (owner ^ which)] * piece
            rows = pl.ds(pl.multiple_of(start, 16), piece)
            in_first = sets_ref[n_blocks + start // block]
            in_last = sets_ref[n_blocks + (start + piece - 1) // block]
            second = second_rows(block, start, (piece, block), in_first, in_last)
            values = source[h * piece : (h + 1) * piece, :]
            for k, kept in enumerate((jnp.where(second, 0.0, values), jnp.where(second, values, 0.0))):
                w_ref[k, 0, rows, :], w_ref[k, 1, rows, :] = split(kept)
    for b in range(n_blocks):
        k = sets_ref[b]
        rows = pl.ds(b * block, block)
        out_ref[rows, :] = -dot3((high_ref[rows, :], low_ref[rows, :]), (w_ref[k, 0], w_ref[k, 1]), (1,))


def rows_terms(block, n_col, n_blocks, sets_ref, z_ref, y, of_sibling):
    start = (lax.axis_index(ROW) * n_col + lax.axis_index(COL)) * y.shape[0]
    second = second_rows(block, start, y.shape, sets_ref[2 * n_blocks], sets_ref[2 * n_blocks + 1])
    kept = second == ((lax.axis_index(ROW) + of_sibling) % 2 == 1)
    return second, dot3(split(jnp.where(kept, z_ref[...], 0.0)), split(y), (0,))


def send_kernel(block, n_col, n_blocks, sets_ref, parts_ref, z_ref, y_ref, send_ref):
    y = parts_ref[0]
    for s in range(1, parts_ref.shape[0]):
        y = y + parts_ref[s]
    y_ref[...] = y
    send_ref[...] = rows_terms(block, n_col, n_blocks, sets_ref, z_ref, y, 1)[1]


def keep_kernel(block, n_col, n_blocks, sets_ref, y_ref, z_ref, keep_ref):
    keep_ref[...] = rows_terms(block, n_col, n_blocks, sets_ref, z_ref, y_ref[...], 0)[1]


def column_kernel(block, n_col, n_blocks, sets_ref, y_ref, column_ref):
    y = y_ref[...]
    start = (lax.axis_index(ROW) * n_col + lax.axis_index(COL)) * y.shape[0]
    second = second_rows(block, start, y.shape, sets_ref[2 * n_blocks], sets_ref[2 * n_blocks + 1])
    column_ref[:, :block] = jnp.where(second, 0.0, y)
    column_ref[:, block:] = jnp.where(second, y, 0.0)


def last_kernel(d_ref, here_ref, there_ref, out_ref):
    core = lax.axis_index(ROW) % 2
    out_ref[core] = d_ref[core] - here_ref[...]
    out_ref[1 - core] = d_ref[1 - core] - there_ref[...]


def per_device(inverse_block, l_panel, d_inverse, owner_map, ancestors):
    block = d_inverse.shape[1]
    rows_dev = l_panel.shape[0]
    n_row = lax.axis_size(ROW)
    n_col = lax.axis_size(COL)
    edge = inverse_block.shape[0]
    n_blocks = edge // block
    n_z = n_row // 2
    f32 = jnp.float32
    smem = pl.BlockSpec(memory_space=pltpu.SMEM)
    vmem = pl.BlockSpec(memory_space=pltpu.VMEM)
    limit = lambda mib: mib * 1024 * 1024
    swap = [(i, i ^ 1) for i in range(n_row)]
    groups = [list(range(c, n_row, 2)) for c in range(2)]

    hbm = pl.BlockSpec(memory_space=pltpu.HBM)
    small = [
        pltpu.SMEM(owner_map.shape, jnp.int32),
        pltpu.SMEM(ancestors.shape, jnp.int32),
    ]
    z = pl.pallas_call(
        functools.partial(pick_kernel, block, n_col),
        out_shape=jax.ShapeDtypeStruct((rows_dev, block), f32),
        in_specs=[hbm, hbm, hbm],
        out_specs=vmem,
        scratch_shapes=[*small, pltpu.VMEM(l_panel.shape, f32), pltpu.SemaphoreType.DMA((3,))],
        compiler_params=pltpu.CompilerParams(vmem_limit_bytes=limit(60)),
    )(owner_map, ancestors, l_panel)
    side, table = place = placement(n_row, n_col)
    targets = {}
    for j in range(n_row):
        for relative, offset in enumerate(table):
            targets[j, source_of(j, offset, side, n_col)] = (j // 2 * 2 + relative) % n_row
    turned = lax.ppermute(z, (ROW, COL), [(j * n_col + s, p * n_col + j) for (j, s), p in targets.items()])
    high, low, sets = pl.pallas_call(
        functools.partial(split_kernel, block, n_col, rows_dev, place),
        out_shape=[
            jax.ShapeDtypeStruct((edge, edge), jnp.bfloat16),
            jax.ShapeDtypeStruct((edge, edge), jnp.bfloat16),
            jax.ShapeDtypeStruct((2 * n_blocks + 2 + n_row,), jnp.int32),
        ],
        in_specs=[hbm, hbm, hbm],
        out_specs=[vmem, vmem, smem],
        scratch_shapes=[*small, pltpu.VMEM((edge, edge), f32), pltpu.SemaphoreType.DMA((n_blocks + 2,))],
        compiler_params=pltpu.CompilerParams(vmem_limit_bytes=limit(44)),
        cost_estimate=pl.CostEstimate(flops=4 * edge * edge, bytes_accessed=8 * edge * edge, transcendentals=0),
    )(owner_map, ancestors, inverse_block)
    turned, high, low, sets = lax.optimization_barrier((turned, high, low, sets))

    def along(x, step):
        pairs = [(2 * q + c, 2 * ((q + step * (1 - 2 * c)) % n_z) + c) for q in range(n_z) for c in range(2)]
        return lax.ppermute(x, ROW, pairs)

    other = lax.ppermute(turned, ROW, swap)
    two, two_other = along(turned, 2), along(other, 2)
    four = along(two, 2)
    chunk, two = lax.optimization_barrier((jnp.concatenate([turned, other]), two))
    one, three = along(chunk, 1), along(jnp.concatenate([two, two_other]), 1)
    held = [[(1, 0), (1, 1)], [(2, 0)], [(2, 1)], [(3, 0), (3, 1)], [(4, 0)]]
    pieces = [one, two, two_other, three, four]
    places = [(0, [(0, 0)]), (0, [(0, 1)])] + [(theirs, h) for theirs in (0, 1) for h in held]
    pieces = [turned, other, *pieces, *(lax.ppermute(p, ROW, swap) for p in pieces)]

    sent = pl.pallas_call(
        functools.partial(product_kernel, block, rows_dev, n_z, places),
        out_shape=jax.ShapeDtypeStruct((edge, block), f32),
        in_specs=[smem, vmem, vmem] + [vmem] * len(pieces),
        out_specs=vmem,
        scratch_shapes=[pltpu.VMEM((2, 2, edge, block), jnp.bfloat16)],
        compiler_params=pltpu.CompilerParams(vmem_limit_bytes=limit(20)),
        cost_estimate=pl.CostEstimate(
            flops=6 * edge * edge * block, bytes_accessed=4 * edge * (edge + 2 * block), transcendentals=0
        ),
    )(sets, high, low, *pieces)
    parts = lax.all_to_all(sent.reshape(n_col, rows_dev, block), COL, 0, 0)

    square = jax.ShapeDtypeStruct((block, block), f32)
    small_limit = pltpu.CompilerParams(vmem_limit_bytes=limit(12))
    y, send = pl.pallas_call(
        functools.partial(send_kernel, block, n_col, n_blocks),
        out_shape=[jax.ShapeDtypeStruct((rows_dev, block), f32), square],
        in_specs=[smem, vmem, vmem],
        out_specs=[vmem, vmem],
        compiler_params=small_limit,
    )(sets, parts, z)
    keep = pl.pallas_call(
        functools.partial(keep_kernel, block, n_col, n_blocks),
        out_shape=square,
        in_specs=[smem, vmem, vmem],
        out_specs=vmem,
        compiler_params=small_limit,
    )(sets, y, z)

    per = block // n_col
    terms = keep + lax.ppermute(send, ROW, swap)
    terms = jnp.sum(lax.all_to_all(terms.reshape(n_col, per, block), COL, 0, 0), axis=0)
    terms = jnp.broadcast_to(terms[None], (n_z, per, block))
    terms = jnp.sum(lax.all_to_all(terms, ROW, 0, 0, axis_index_groups=groups), axis=0)
    terms = jnp.broadcast_to(terms[None], (n_col, per, block))
    here = lax.all_to_all(terms, COL, 0, 0).reshape(block, block)
    there = lax.ppermute(here, ROW, swap)
    y, here = lax.optimization_barrier((y, here))
    column = pl.pallas_call(
        functools.partial(column_kernel, block, n_col, n_blocks),
        out_shape=jax.ShapeDtypeStruct((rows_dev, 2 * block), f32),
        in_specs=[smem, vmem],
        out_specs=vmem,
        compiler_params=small_limit,
    )(sets, y)
    there, column = lax.optimization_barrier((there, column))
    diag = pl.pallas_call(
        last_kernel,
        out_shape=jax.ShapeDtypeStruct(d_inverse.shape, f32),
        in_specs=[vmem, vmem, vmem],
        out_specs=vmem,
        compiler_params=small_limit,
    )(d_inverse, here, there)
    return column, diag


def solution(mesh):
    return jax.shard_map(
        per_device,
        mesh=mesh,
        in_specs=(P(ROW, COL), P((ROW, COL), None), P(), P(), P()),
        out_specs=(P((ROW, COL), None), P()),
        check_vma=False,
    )
```
